512 devices in a mesh: section: 4 (over x), ctx: 128 (over z, y, core).
Axes of the slice: x: 4, y: 8, z: 8, core: 2. Of those that a mesh axis runs over, the one named last changes fastest.
Arguments:
- gate_values: bfloat16 [4, 16384, 4096], P('section', 'ctx'), may hold values from -6 to 6
- conv_input: bfloat16 [4, 16384, 4096], P('section', 'ctx'), may hold values from -6 to 6
- sent_grads: bfloat16 [4, 16384, 4096], P('section', 'ctx'), may hold values from -6 to 6
- filter_taps: float32 [4, 256, 128], P('section'), may hold values from -0.5 to 0.5
- doc_lengths: int32 [4, 128], P('section'), may hold values from 1 to 512, 16384 in all within a row
Outputs:
- input_grad: bfloat16 [4, 16384, 4096], P('section', 'ctx')
- filter_grad: float32 [4, 256, 128], P('section')
The draws below stay inside these ranges and needn't reach their ends.
Inputs may be any that keep to these rules, and one draw needn't show every extreme that they name: `doc_lengths`: each row sums to 16384; its largest length is exactly 512.
All inputs are finite; a program needn't handle non-finite values.
Results may differ from the reference program's by a relative error of at most 0.011.
Values may be sent and summed in bfloat16 or wider, within the bound.
No kernel may reach another device: no remote copies, remote signals or barrier semaphores. Data moves between devices by JAX's collectives and lax.ppermute only.
A program may use at most 64 MiB of HBM per device.

```python
import math
import jax
import jax.numpy as jnp
import numpy as np
from jax import lax

D = 4096
GROUP = 16
L = 128
TOK_DEV = 128
FILTERS = 256
TOKENS = 16384
DOCS = 128
SECTIONS = 4


def steps_of(stream_key, extent, shards, least, largest):
    gain, own = 1.0, jax.random.fold_in(stream_key, 6)
    for position, shards_of in shards:
        heights = jnp.exp(jax.random.uniform(jax.random.fold_in(own, position), (shards_of,), jnp.float32, least / len(shards), largest / len(shards)))
        gain = gain * jnp.repeat(heights, extent[position] // shards_of).reshape([-1 if axis == position else 1 for axis in range(len(extent))])
    return gain


def profile(count, total, reach, lean):
    weights = [(1 << 20) // math.isqrt(rank ** lean) + 1 for rank in range(2, count + 1)]
    spare, given = total - reach - (count - 1), [1] * (count - 1)
    while spare > 0:
        movable = [i for i in range(count - 1) if given[i] < reach]
        mass, remaining = sum([weights[i] for i in movable]), spare
        for i in movable:
            more = min(reach - given[i], max(1, remaining * weights[i] // mass), spare)
            given[i] = given[i] + more
            spare = spare - more
    return np.array([reach] + given)


def uneven_parts(rng, count, total, most, slope):
    if count == 2:
        one = jax.random.randint(rng, (), max(1, total - most), min(most, total - 1) + 1)
        return jnp.stack([one, total - one])
    tallies = jnp.asarray(profile(count, total, most, slope), jnp.int32)
    couples = (count - 1) // 2
    giver, receiver = tallies[1:1 + 2 * couples:2], tallies[2:2 + 2 * couples:2]
    room = jnp.minimum(giver - 1, most - receiver)
    moved = jax.random.randint(jax.random.fold_in(rng, 1), (couples,), 0, 1 << 20) % (room + 1)
    tallies = tallies.at[1:1 + 2 * couples:2].set(giver - moved).at[2:2 + 2 * couples:2].set(receiver + moved)
    return tallies[jax.random.permutation(jax.random.fold_in(rng, 2), count)]


def bell_draw(rng, dims, deviation, limit, cuts=(), kind=jnp.bfloat16):
    array = deviation * jax.random.normal(rng, dims, jnp.float32)
    if cuts:
        array = array * steps_of(rng, dims, cuts, -0.22, 0.18)
    return jnp.clip(array, -limit, limit).astype(kind)


def setup_inputs(seed: int = 0) -> dict:
    key_of = jax.random.split(jax.random.key(seed), 6)
    return {
        "gate_values": bell_draw(key_of[0], (SECTIONS, TOKENS, D), 1.0, 6.0, ((0, 4), (1, 128))),
        "conv_input": bell_draw(key_of[1], (SECTIONS, TOKENS, D), 1.0, 6.0, ((0, 4), (1, 128))),
        "sent_grads": bell_draw(key_of[2], (SECTIONS, TOKENS, D), 1.0, 6.0, ((0, 4), (1, 128))),
        "filter_taps": bell_draw(key_of[3], (SECTIONS, FILTERS, L), L ** -0.5, 0.5, ((0, 4),), jnp.float32),
        "doc_lengths": jax.vmap(lambda own: uneven_parts(own, DOCS, TOKENS, 4 * TOK_DEV, 2))(jax.random.split(key_of[4], SECTIONS)).reshape((SECTIONS, DOCS)).astype(jnp.int32),
    }


def one_section(gate_rows, input_rows, arrived, taps_section, lengths_section):
    scaled = (arrived.astype(jnp.float32) * gate_rows.astype(jnp.float32)).astype(jnp.bfloat16)
    doc_bounds = jnp.cumsum(lengths_section).astype(jnp.int32)
    positions = jnp.arange(TOKENS, dtype=jnp.int32)
    doc_end = jnp.min(jnp.where(doc_bounds[None, :] > positions[:, None], doc_bounds[None, :], TOKENS), axis=1)
    taps_channel = jnp.repeat(taps_section.astype(jnp.bfloat16).astype(jnp.float32), GROUP, axis=0)
    padded = jnp.pad(scaled.astype(jnp.float32), ((0, L), (0, 0)))
    source = input_rows.astype(jnp.float32)

    def accumulate(offset, carried):
        grad_rows, grad_taps = carried
        shifted = lax.dynamic_slice(padded, (offset, 0), (TOKENS, D))
        valid = (positions + offset < doc_end).astype(jnp.float32)[:, None]
        term = shifted * valid
        column_taps = lax.dynamic_index_in_dim(taps_channel, offset, 1, keepdims=False)
        grad_rows = grad_rows + term * column_taps[None, :]
        column = jnp.sum(term * source, axis=0).reshape(FILTERS, GROUP).sum(axis=1)
        grad_taps = lax.dynamic_update_slice(grad_taps, column[:, None], (0, offset))
        return grad_rows, grad_taps

    start = (jnp.zeros((TOKENS, D), jnp.float32), jnp.zeros((FILTERS, L), jnp.float32))
    grad_rows, grad_taps = lax.fori_loop(0, L, accumulate, start)
    return grad_rows.astype(jnp.bfloat16), grad_taps


def reference(gate_values, conv_input, sent_grads, filter_taps, doc_lengths):
    grads_in = []
    grads_taps = []
    for section_index in range(SECTIONS):
        arrived = sent_grads[(section_index + 1) % SECTIONS]
        grad_rows, grad_taps = one_section(gate_values[section_index], conv_input[section_index], arrived, filter_taps[section_index], doc_lengths[section_index])
        grads_in.append(grad_rows)
        grads_taps.append(grad_taps)
    return jnp.stack(grads_in), jnp.stack(grads_taps)
```

```python
import functools
import jax
import jax.numpy as jnp
from jax import lax
from jax.experimental import pallas as pl
from jax.experimental.pallas import tpu as pltpu
from jax.sharding import PartitionSpec as P

BF, F32 = jnp.bfloat16, jnp.float32
TOK, CH, GRP, TAPS, FILT = 128, 4096, 16, 128, 256
VMEM = pl.BlockSpec(memory_space=pltpu.VMEM)
ROOM = 16 * 1024 * 1024


def lag_sums(products, flip):
    hi = products.astype(BF)
    lo = (products - hi.astype(F32)).astype(BF)
    flipped = jnp.dot(hi, flip, preferred_element_type=F32) + jnp.dot(lo, flip, preferred_element_type=F32)
    rows = []
    for g in range(products.shape[0] // 8):
        one = pltpu.roll(flipped[8 * g : 8 * g + 8], 0, 1, stride=1, stride_axis=0)
        rows.append(jnp.sum(one, axis=0, keepdims=True))
    return jnp.concatenate(rows, axis=0)


def taps_kernel(start, arr_ref, gate_ref, beh_ref, own_ref, mask_ref, *rest):
    acc_ref = rest[-1]
    width = arr_ref.shape[1]
    mask = mask_ref[...]
    row = lax.broadcasted_iota(jnp.int32, (TOK, TOK), 0)
    lane = lax.broadcasted_iota(jnp.int32, (TOK, TOK), 1)
    tri = lane <= row
    flip = ((row + lane) % TAPS == 0).astype(F32).astype(BF)
    chosen = (lane[:8] // GRP == row[:8]).astype(F32).astype(BF)
    s_ref, g_ref = rest[-3:-1]
    for h in range(width // 128):
        here = slice(128 * h, 128 * h + 128)
        there = slice(start + 128 * h, start + 128 * h + 128)
        s = (arr_ref[:, here].astype(F32) * gate_ref[:, there].astype(F32)).astype(BF)
        s_ref[:, here] = s
        past = jnp.concatenate([beh_ref[:, here], own_ref[:, there]], axis=0)
        for g in range(8):
            one = s * chosen[g : g + 1, :]
            prod = lax.dot_general(one, past, (((1,), (1,)), ((), ())), preferred_element_type=F32)
            both = jnp.where(tri, prod[:, 128:], prod[:, :128]) * mask
            part = both[0:8]
            for a in range(1, 16):
                part = part + pltpu.roll(both[8 * a : 8 * a + 8], 128 - 8 * a, 1)
            acc_ref[64 * h + 8 * g : 64 * h + 8 * g + 8, :] = part
    sums = lag_sums(acc_ref[...], flip)
    if len(g_ref.shape) == 2:
        g_ref[...] = sums
    else:
        whole = jnp.concatenate([r[...] for r in rest[:-3]] + [sums], axis=0)
        n, per = g_ref.shape[:2]
        for i in range(n):
            g_ref[i] = whole[per * i : per * i + per].astype(BF)


def taps_block(arr, gate, behind, own, mask, start, before=(), parts=None):
    width = arr.shape[1]
    if parts:
        sums = jax.ShapeDtypeStruct((parts, FILT // parts, TAPS), BF)
    else:
        sums = jax.ShapeDtypeStruct((width // GRP, TAPS), F32)
    args = (arr, gate, *behind, own, mask, *before)
    return pl.pallas_call(
        functools.partial(taps_kernel, start),
        in_specs=[VMEM] * len(args),
        out_specs=[VMEM, VMEM],
        out_shape=[jax.ShapeDtypeStruct((TOK, width), BF), sums],
        scratch_shapes=[pltpu.VMEM((width // 2, 128), F32)],
        compiler_params=pltpu.CompilerParams(vmem_limit_bytes=ROOM),
        cost_estimate=pl.CostEstimate(flops=1 << 56, bytes_accessed=width << 11, transcendentals=0),
        name=f"taps_block_{start}",
    )(*args)


def rows_kernel(start, offset, width, s_ref, ahead_ref, taps_ref, mask_ref, *rest):
    o_ref, block, sem = rest[-3:]
    mask = mask_ref[...]
    lane = lax.broadcasted_iota(jnp.int32, (TOK, 128), 1) // GRP
    for h in range(width // 128):
        here = slice(128 * h, 128 * h + 128)
        there = slice(offset + 128 * h, offset + 128 * h + 128)
        ext = jnp.concatenate([s_ref[:, there], ahead_ref[:, there]], axis=0)
        acc = None
        for g in range(8):
            f = (start + 128 * h) // GRP + g
            base = jnp.broadcast_to(taps_ref[f : f + 1, :], (8, 128))
            base = pltpu.roll(base, 0, 1, stride=1, stride_axis=0)
            circ = jnp.concatenate([base] + [pltpu.roll(base, 8 * a, 1) for a in range(1, 16)], axis=0).astype(BF)
            toep = jnp.concatenate([circ, circ], axis=1) * mask
            prod = jnp.dot(toep, ext, preferred_element_type=F32)
            acc = prod if acc is None else jnp.where(lane == g, prod, acc)
        block[:, here] = acc.astype(BF)
    copy = pltpu.make_async_copy(block, o_ref.at[:, pl.ds(start, width)], sem)
    copy.start()
    copy.wait()


def rows_block(scaled, ahead, taps, mask, out, start, offset, width):
    specs = [VMEM] * 4
    args = [scaled, ahead, taps, mask]
    if out is not None:
        specs.append(pl.BlockSpec(memory_space=pl.ANY))
        args.append(out)
    return pl.pallas_call(
        functools.partial(rows_kernel, start, offset, width),
        in_specs=specs,
        out_specs=pl.BlockSpec(memory_space=pl.ANY),
        out_shape=jax.ShapeDtypeStruct((TOK, CH), BF),
        input_output_aliases={4: 0} if out is not None else {},
        scratch_shapes=[pltpu.VMEM((TOK, width), BF), pltpu.SemaphoreType.DMA(())],
        compiler_params=pltpu.CompilerParams(vmem_limit_bytes=ROOM),
        cost_estimate=pl.CostEstimate(flops=width << 18, bytes_accessed=width << 10, transcendentals=0),
        name=f"rows_block_{start}",
    )(*args)


def sum_kernel(parts_ref, o_ref):
    total = parts_ref[0].astype(F32)
    for i in range(1, parts_ref.shape[0]):
        total = total + parts_ref[i].astype(F32)
    total = total.astype(BF)
    for i in range(o_ref.shape[0]):
        o_ref[i] = total


def summed(parts, copies):
    return pl.pallas_call(
        sum_kernel,
        in_specs=[VMEM],
        out_specs=VMEM,
        out_shape=jax.ShapeDtypeStruct((copies,) + parts.shape[1:], BF),
        compiler_params=pltpu.CompilerParams(vmem_limit_bytes=ROOM),
        cost_estimate=pl.CostEstimate(flops=1 << 56, bytes_accessed=parts.size * 2, transcendentals=0),
        name=f"sum_of_{parts.shape[0]}",
    )(parts)


def cut_kernel(whole_ref, *rest):
    n = len(rest) // 2
    copies, at = [], 0
    for i in range(n):
        width = rest[i].shape[1]
        copies.append(pltpu.make_async_copy(whole_ref.at[:, pl.ds(at, width)], rest[i], rest[n + i]))
        at += width
    for copy in copies:
        copy.start()
    for copy in copies:
        copy.wait()


def cut(whole, widths):
    return pl.pallas_call(
        cut_kernel,
        in_specs=[pl.BlockSpec(memory_space=pltpu.HBM)],
        out_specs=[VMEM] * len(widths),
        out_shape=[jax.ShapeDtypeStruct((TOK, w), BF) for w in widths],
        scratch_shapes=[pltpu.SemaphoreType.DMA(()) for _ in widths],
        compiler_params=pltpu.CompilerParams(vmem_limit_bytes=56 * 1024 * 1024),
        name="cut",
    )(whole)


def mask_kernel(base_ref, len_ref, ahead_ref, behind_ref):
    row = lax.broadcasted_iota(jnp.int32, (128, 128), 0)
    col = lax.broadcasted_iota(jnp.int32, (128, 128), 1)
    upto = (row <= col).astype(F32).astype(BF)
    lengths = jnp.broadcast_to(len_ref[...], (8, 128))
    high = lengths // 16
    low = lengths - 16 * high
    bounds = 16.0 * jnp.dot(high.astype(F32).astype(BF), upto, preferred_element_type=F32)
    bounds = bounds + jnp.dot(low.astype(F32).astype(BF), upto, preferred_element_type=F32)
    bounds = jnp.broadcast_to(bounds[0:1, :], (TOK, 128))
    base = base_ref[0, 0]
    here = (base + row).astype(F32)
    ended = bounds <= here
    end = jnp.min(jnp.where(ended, 2.0 * CH * TAPS, bounds), axis=1, keepdims=True)
    begin = jnp.max(jnp.where(ended, bounds, 0.0), axis=1, keepdims=True)
    source = base + jnp.where(col <= row, col, col - TOK)
    behind_ref[...] = (source.astype(F32) >= begin).astype(F32)
    own = (base + col).astype(F32)
    ahead_ref[:, :TOK] = jnp.where((col >= row) & (own < end), 1.0, 0.0).astype(BF)
    ahead_ref[:, TOK:] = jnp.where((col < row) & (own + 1.0 * TOK < end), 1.0, 0.0).astype(BF)


def masks(doc_lengths, base):
    return pl.pallas_call(
        mask_kernel,
        in_specs=[pl.BlockSpec(memory_space=pltpu.SMEM), VMEM],
        out_specs=[VMEM, VMEM],
        out_shape=[jax.ShapeDtypeStruct((TOK, 2 * TOK), BF), jax.ShapeDtypeStruct((TOK, TOK), F32)],
        compiler_params=pltpu.CompilerParams(vmem_limit_bytes=ROOM),
        name="masks",
    )(base.reshape(1, 1), doc_lengths.reshape(1, 128))


def last_sum_kernel(rows, parts_ref, o_ref):
    sets = FILT // rows
    for r in range(sets):
        total = parts_ref[r].astype(F32)
        for i in range(r + sets, parts_ref.shape[0], sets):
            total = total + parts_ref[i].astype(F32)
        o_ref[rows * r : rows * r + rows, :] = total


def last_sum(parts):
    return pl.pallas_call(
        functools.partial(last_sum_kernel, parts.shape[1]),
        in_specs=[VMEM],
        out_specs=VMEM,
        out_shape=jax.ShapeDtypeStruct((FILT, TAPS), F32),
        compiler_params=pltpu.CompilerParams(vmem_limit_bytes=ROOM),
        name="last_sum",
    )(parts)


WIDTHS = (2048, 2048)


def place(z, y, c):
    return (z * 8 + y) * 2 + c


PLANES = [[place(z + i, y, c) for i in range(2) for y in range(8) for c in range(2)] for z in range(0, 8, 2)]


def shifted(value, axis, steps):
    count = lax.axis_size(axis)
    return lax.ppermute(value, axis, [(i, (i + steps) % count) for i in range(count)])


def exchanged(value, groups):
    return lax.all_to_all(value, "ctx", 0, 0, axis_index_groups=groups)


def tied(value, *after):
    return lax.optimization_barrier((value, *after))[0]


def on_device(gate_values, conv_input, sent_grads, filter_taps, doc_lengths):
    gate, conv, sent, taps = gate_values[0], conv_input[0], sent_grads[0], filter_taps[0]
    base = lax.axis_index("ctx") * TOK
    w0, w1 = WIDTHS
    piece0, piece1 = cut(sent, WIDTHS)
    arr0 = shifted(piece0, "section", -1)
    arr1 = shifted(piece1, "section", -1)
    behind = [shifted(piece, "ctx", 1) for piece in cut(tied(conv, piece0), (CH // 2, CH // 2))]
    ahead_mask, behind_mask = masks(tied(doc_lengths, arr0), base)
    s0, g0 = taps_block(arr0, gate, behind[:1], conv, behind_mask, 0)
    ahead0 = shifted(s0, "ctx", -1)
    s1, local = taps_block(arr1, gate, behind[1:], conv, behind_mask, w0, (g0,), 32)
    got = exchanged(local, PLANES)
    ahead1 = shifted(s1, "ctx", -1)
    out = rows_block(s0, ahead0, taps, ahead_mask, None, 0, 0, 1024)
    got = exchanged(summed(tied(got, out), 128), None)
    out = rows_block(s0, ahead0, taps, ahead_mask, out, 1024, 1024, w0 - 1024)
    out = rows_block(s1, ahead1, taps, ahead_mask, out, w0, 0, w1)
    filter_grad = last_sum(tied(got, out))[None]
    return out[None], filter_grad


def solution(mesh):
    return jax.shard_map(
        on_device,
        mesh=mesh,
        in_specs=(
            P("section", "ctx", None),
            P("section", "ctx", None),
            P("section", "ctx", None),
            P("section", None, None),
            P("section", None),
        ),
        out_specs=(P("section", "ctx", None), P("section", None, None)),
        check_vma=False,
    )
```

```python
import functools
import jax
import jax.numpy as jnp
from jax import lax
from jax.experimental import pallas as pl
from jax.experimental.pallas import tpu as pltpu
from jax.sharding import PartitionSpec as P

BF, F32 = jnp.bfloat16, jnp.float32
TOK, CH, GRP, TAPS, FILT = 128, 4096, 16, 128, 256
VMEM = pl.BlockSpec(memory_space=pltpu.VMEM)
ROOM = 12 * 1024 * 1024


def lag_sums(products, flip):
    hi = products.astype(BF)
    lo = (products - hi.astype(F32)).astype(BF)
    flipped = jnp.dot(hi, flip, preferred_element_type=F32) + jnp.dot(lo, flip, preferred_element_type=F32)
    rows = []
    for g in range(products.shape[0] // 8):
        one = pltpu.roll(flipped[8 * g : 8 * g + 8], 0, 1, stride=1, stride_axis=0)
        rows.append(jnp.sum(one, axis=0, keepdims=True))
    return jnp.concatenate(rows, axis=0)


def taps_kernel(arr_ref, gate_ref, beh_ref, own_ref, mask_ref, s0_ref, s1_ref, g_ref, acc_ref):
    mask = mask_ref[...]
    row = lax.broadcasted_iota(jnp.int32, (TOK, TOK), 0)
    lane = lax.broadcasted_iota(jnp.int32, (TOK, TOK), 1)
    tri = lane <= row
    flip = ((row + lane) % TAPS == 0).astype(F32).astype(BF)
    chosen = (lane[:8] // GRP == row[:8]).astype(F32).astype(BF)
    for h in range(CH // 128):
        here = slice(128 * h, 128 * h + 128)
        s = (arr_ref[:, here].astype(F32) * gate_ref[:, here].astype(F32)).astype(BF)
        s_ref = s0_ref if h < CH // 256 else s1_ref
        at = 128 * h % (CH // 2)
        s_ref[:, at : at + 128] = s
        past = jnp.concatenate([beh_ref[:, here], own_ref[:, here]], axis=0)
        for g in range(8):
            one = s * chosen[g : g + 1, :]
            prod = lax.dot_general(one, past, (((1,), (1,)), ((), ())), preferred_element_type=F32)
            both = jnp.where(tri, prod[:, 128:], prod[:, :128]) * mask
            part = both[0:8]
            for a in range(1, 16):
                part = part + pltpu.roll(both[8 * a : 8 * a + 8], 128 - 8 * a, 1)
            acc_ref[64 * h + 8 * g : 64 * h + 8 * g + 8, :] = part
    sums = lag_sums(acc_ref[...], flip)
    per = g_ref.shape[1]
    for i in range(g_ref.shape[0]):
        g_ref[i] = sums[per * i : per * i + per].astype(BF)


def taps_sums(arr, gate, behind, own, mask, parts):
    half = jax.ShapeDtypeStruct((TOK, CH // 2), BF)
    return pl.pallas_call(
        taps_kernel,
        in_specs=[VMEM] * 5,
        out_specs=[VMEM] * 3,
        out_shape=[half, half, jax.ShapeDtypeStruct((parts, FILT // parts, TAPS), BF)],
        scratch_shapes=[pltpu.VMEM((CH // 2, 128), F32)],
        compiler_params=pltpu.CompilerParams(vmem_limit_bytes=ROOM),
        cost_estimate=pl.CostEstimate(flops=CH << 18, bytes_accessed=CH << 11, transcendentals=0),
        name="taps_sums",
    )(arr, gate, behind, own, mask)


def rows_kernel(start, offset, width, s_ref, ahead_ref, taps_ref, mask_ref, *rest):
    o_ref, block, sem = rest[-3:]
    mask = mask_ref[...]
    lane = lax.broadcasted_iota(jnp.int32, (TOK, 128), 1) // GRP
    for h in range(width // 128):
        here = slice(128 * h, 128 * h + 128)
        there = slice(offset + 128 * h, offset + 128 * h + 128)
        ext = jnp.concatenate([s_ref[:, there], ahead_ref[:, there]], axis=0)
        acc = None
        for g in range(8):
            f = (start + 128 * h) // GRP + g
            base = jnp.broadcast_to(taps_ref[f : f + 1, :], (8, 128))
            base = pltpu.roll(base, 0, 1, stride=1, stride_axis=0)
            circ = jnp.concatenate([base] + [pltpu.roll(base, 8 * a, 1) for a in range(1, 16)], axis=0).astype(BF)
            toep = jnp.concatenate([circ, circ], axis=1) * mask
            prod = jnp.dot(toep, ext, preferred_element_type=F32)
            acc = prod if acc is None else jnp.where(lane == g, prod, acc)
        block[:, here] = acc.astype(BF)
    copy = pltpu.make_async_copy(block, o_ref.at[:, pl.ds(start, width)], sem)
    copy.start()
    copy.wait()


def rows_block(scaled, ahead, taps, mask, out, start, offset, width):
    specs = [VMEM] * 4
    args = [scaled, ahead, taps, mask]
    if out is not None:
        specs.append(pl.BlockSpec(memory_space=pl.ANY))
        args.append(out)
    return pl.pallas_call(
        functools.partial(rows_kernel, start, offset, width),
        in_specs=specs,
        out_specs=pl.BlockSpec(memory_space=pl.ANY),
        out_shape=jax.ShapeDtypeStruct((TOK, CH), BF),
        input_output_aliases={4: 0} if out is not None else {},
        scratch_shapes=[pltpu.VMEM((TOK, width), BF), pltpu.SemaphoreType.DMA(())],
        compiler_params=pltpu.CompilerParams(vmem_limit_bytes=ROOM),
        cost_estimate=pl.CostEstimate(flops=1 << 35, bytes_accessed=width << 10, transcendentals=0),
        name=f"rows_block_{start}",
    )(*args)


def sum_kernel(parts_ref, o_ref):
    total = parts_ref[0].astype(F32)
    for i in range(1, parts_ref.shape[0]):
        total = total + parts_ref[i].astype(F32)
    total = total.astype(BF)
    for i in range(o_ref.shape[0]):
        o_ref[i] = total


def summed(parts, copies):
    return pl.pallas_call(
        sum_kernel,
        in_specs=[VMEM],
        out_specs=VMEM,
        out_shape=jax.ShapeDtypeStruct((copies,) + parts.shape[1:], BF),
        compiler_params=pltpu.CompilerParams(vmem_limit_bytes=ROOM),
        cost_estimate=pl.CostEstimate(flops=1 << 35, bytes_accessed=parts.size * 2, transcendentals=0),
        name=f"sum_of_{parts.shape[0]}",
    )(parts)


def held_kernel(gate_ref, own_ref, gate_out, own_out, sems):
    copies = [
        pltpu.make_async_copy(gate_ref, gate_out, sems.at[0]),
        pltpu.make_async_copy(own_ref, own_out, sems.at[1]),
    ]
    for copy in copies:
        copy.start()
    for copy in copies:
        copy.wait()


def held(gate, own):
    block = jax.ShapeDtypeStruct((TOK, CH), BF)
    return pl.pallas_call(
        held_kernel,
        in_specs=[pl.BlockSpec(memory_space=pltpu.HBM)] * 2,
        out_specs=[VMEM] * 2,
        out_shape=[block, block],
        scratch_shapes=[pltpu.SemaphoreType.DMA((2,))],
        compiler_params=pltpu.CompilerParams(vmem_limit_bytes=4 * 1024 * 1024),
        cost_estimate=pl.CostEstimate(flops=1 << 30, bytes_accessed=4 << 20, transcendentals=0),
        name="held",
    )(gate, own)


def mask_kernel(base_ref, len_ref, ahead_ref, behind_ref):
    row = lax.broadcasted_iota(jnp.int32, (128, 128), 0)
    col = lax.broadcasted_iota(jnp.int32, (128, 128), 1)
    upto = (row <= col).astype(F32).astype(BF)
    lengths = jnp.broadcast_to(len_ref[...], (8, 128))
    high = lengths // 16
    low = lengths - 16 * high
    bounds = 16.0 * jnp.dot(high.astype(F32).astype(BF), upto, preferred_element_type=F32)
    bounds = bounds + jnp.dot(low.astype(F32).astype(BF), upto, preferred_element_type=F32)
    bounds = jnp.broadcast_to(bounds[0:1, :], (TOK, 128))
    base = base_ref[0, 0]
    here = (base + row).astype(F32)
    ended = bounds <= here
    end = jnp.min(jnp.where(ended, 2.0 * CH * TAPS, bounds), axis=1, keepdims=True)
    begin = jnp.max(jnp.where(ended, bounds, 0.0), axis=1, keepdims=True)
    source = base + jnp.where(col <= row, col, col - TOK)
    behind_ref[...] = (source.astype(F32) >= begin).astype(F32)
    own = (base + col).astype(F32)
    ahead_ref[:, :TOK] = jnp.where((col >= row) & (own < end), 1.0, 0.0).astype(BF)
    ahead_ref[:, TOK:] = jnp.where((col < row) & (own + 1.0 * TOK < end), 1.0, 0.0).astype(BF)


def masks(doc_lengths, base):
    return pl.pallas_call(
        mask_kernel,
        in_specs=[pl.BlockSpec(memory_space=pltpu.SMEM), VMEM],
        out_specs=[VMEM, VMEM],
        out_shape=[jax.ShapeDtypeStruct((TOK, 2 * TOK), BF), jax.ShapeDtypeStruct((TOK, TOK), F32)],
        compiler_params=pltpu.CompilerParams(vmem_limit_bytes=ROOM),
        name="masks",
    )(base.reshape(1, 1), doc_lengths.reshape(1, 128))


def last_sum_kernel(rows, parts_ref, o_ref):
    sets = FILT // rows
    for r in range(sets):
        total = parts_ref[r].astype(F32)
        for i in range(r + sets, parts_ref.shape[0], sets):
            total = total + parts_ref[i].astype(F32)
        o_ref[rows * r : rows * r + rows, :] = total


def last_sum(parts):
    return pl.pallas_call(
        functools.partial(last_sum_kernel, parts.shape[1]),
        in_specs=[VMEM],
        out_specs=VMEM,
        out_shape=jax.ShapeDtypeStruct((FILT, TAPS), F32),
        compiler_params=pltpu.CompilerParams(vmem_limit_bytes=ROOM),
        name="last_sum",
    )(parts)


def place(z, y, c):
    return (z * 8 + y) * 2 + c


PLANES = [[place(z + i, y, c) for i in range(2) for y in range(8) for c in range(2)] for z in range(0, 8, 2)]


def shifted(value, axis, steps, around=False):
    count = lax.axis_size(axis)
    pairs = [(i, i + steps) for i in range(count)]
    pairs = [(i, j % count) for i, j in pairs if around or 0 <= j < count]
    return lax.ppermute(value, axis, pairs)


def exchanged(value, groups):
    return lax.all_to_all(value, "ctx", 0, 0, axis_index_groups=groups)


def tied(value, *after):
    return lax.optimization_barrier((value, *after))[0]


def on_device(gate_values, conv_input, sent_grads, filter_taps, doc_lengths):
    gate, conv, sent, taps = gate_values[0], conv_input[0], sent_grads[0], filter_taps[0]
    base = lax.axis_index("ctx") * TOK
    half = CH // 2
    arrived = shifted(sent, "section", -1, around=True)
    behind = shifted(conv, "ctx", 1)
    gate, own = held(gate, conv)
    ahead_mask, behind_mask = masks(tied(doc_lengths, arrived), base)
    s0, s1, local = taps_sums(arrived, gate, behind, own, behind_mask, 32)
    got = exchanged(local, PLANES)
    ahead0 = shifted(s0, "ctx", -1)
    ahead1 = shifted(s1, "ctx", -1)
    got = exchanged(summed(got, 128), None)
    out = rows_block(s0, ahead0, taps, ahead_mask, None, 0, 0, half)
    out = rows_block(s1, ahead1, taps, ahead_mask, out, half, 0, half)
    filter_grad = last_sum(tied(got, out))[None]
    return out[None], filter_grad


def solution(mesh):
    return jax.shard_map(
        on_device,
        mesh=mesh,
        in_specs=(
            P("section", "ctx", None),
            P("section", "ctx", None),
            P("section", "ctx", None),
            P("section", None, None),
            P("section", None),
        ),
        out_specs=(P("section", "ctx", None), P("section", None, None)),
        check_vma=False,
    )
```

```python
import functools
import jax
import jax.numpy as jnp
from jax import lax
from jax.experimental import pallas as pl
from jax.experimental.pallas import tpu as pltpu
from jax.sharding import PartitionSpec as P

BF, F32 = jnp.bfloat16, jnp.float32
TOK, CH, GRP, TAPS, FILT = 128, 4096, 16, 128, 256
VMEM = pl.BlockSpec(memory_space=pltpu.VMEM)
ROOM = 12 * 1024 * 1024


def lag_sums(products_ref, flip):
    count = products_ref.shape[0] // 8
    total = products_ref[pl.ds(0, count, stride=8), :]
    for b in range(1, 8):
        total = total + pltpu.roll(products_ref[pl.ds(b, count, stride=8), :], TAPS - b, 1)
    hi = total.astype(BF)
    lo = (total - hi.astype(F32)).astype(BF)
    return jnp.dot(hi, flip, preferred_element_type=F32) + jnp.dot(lo, flip, preferred_element_type=F32)


def taps_kernel(arr_ref, gate_ref, beh_ref, own_ref, mask_ref, s0_ref, s1_ref, g_ref, acc_ref):
    mask = mask_ref[...]
    row = lax.broadcasted_iota(jnp.int32, (TOK, TOK), 0)
    lane = lax.broadcasted_iota(jnp.int32, (TOK, TOK), 1)
    tri = lane <= row
    flip = ((row + lane) % TAPS == 0).astype(F32).astype(BF)
    chosen = (lane[:8] // GRP == row[:8]).astype(F32).astype(BF)
    for h in range(CH // 128):
        here = slice(128 * h, 128 * h + 128)
        s = (arr_ref[:, here].astype(F32) * gate_ref[:, here].astype(F32)).astype(BF)
        s_ref = s0_ref if h < CH // 256 else s1_ref
        at = 128 * h % (CH // 2)
        s_ref[:, at : at + 128] = s
        past = jnp.concatenate([beh_ref[:, here], own_ref[:, here]], axis=0)
        for g in range(8):
            one = s * chosen[g : g + 1, :]
            prod = lax.dot_general(one, past, (((1,), (1,)), ((), ())), preferred_element_type=F32)
            both = jnp.where(tri, prod[:, 128:], prod[:, :128]) * mask
            part = both[0:8]
            for a in range(1, 16):
                part = part + pltpu.roll(both[8 * a : 8 * a + 8], 128 - 8 * a, 1)
            acc_ref[64 * h + 8 * g : 64 * h + 8 * g + 8, :] = part
    sums = lag_sums(acc_ref, flip)
    per = g_ref.shape[1]
    for i in range(g_ref.shape[0]):
        g_ref[i] = sums[per * i : per * i + per].astype(BF)


def taps_sums(arr, gate, behind, own, mask, parts):
    half = jax.ShapeDtypeStruct((TOK, CH // 2), BF)
    return pl.pallas_call(
        taps_kernel,
        in_specs=[VMEM] * 5,
        out_specs=[VMEM] * 3,
        out_shape=[half, half, jax.ShapeDtypeStruct((parts, FILT // parts, TAPS), BF)],
        scratch_shapes=[pltpu.VMEM((CH // 2, 128), F32)],
        compiler_params=pltpu.CompilerParams(vmem_limit_bytes=ROOM),
        cost_estimate=pl.CostEstimate(flops=CH << 18, bytes_accessed=CH << 11, transcendentals=0),
        name="taps_sums",
    )(arr, gate, behind, own, mask)


def rows_kernel(start, offset, width, s_ref, ahead_ref, taps_ref, mask_ref, *rest):
    o_ref, block, sem = rest[-3:]
    mask = mask_ref[...]
    lane = lax.broadcasted_iota(jnp.int32, (TOK, 128), 1) // GRP
    for h in range(width // 128):
        here = slice(128 * h, 128 * h + 128)
        there = slice(offset + 128 * h, offset + 128 * h + 128)
        ext = jnp.concatenate([s_ref[:, there], ahead_ref[:, there]], axis=0)
        acc = None
        for g in range(8):
            f = (start + 128 * h) // GRP + g
            base = jnp.broadcast_to(taps_ref[f : f + 1, :], (8, 128))
            base = pltpu.roll(base, 0, 1, stride=1, stride_axis=0)
            circ = jnp.concatenate([base] + [pltpu.roll(base, 8 * a, 1) for a in range(1, 16)], axis=0).astype(BF)
            toep = jnp.concatenate([circ, circ], axis=1) * mask
            prod = jnp.dot(toep, ext, preferred_element_type=F32)
            acc = prod if acc is None else jnp.where(lane == g, prod, acc)
        block[:, here] = acc.astype(BF)
    copy = pltpu.make_async_copy(block, o_ref.at[:, pl.ds(start, width)], sem)
    copy.start()
    copy.wait()


def rows_block(scaled, ahead, taps, mask, out, start, offset, width):
    specs = [VMEM] * 4
    args = [scaled, ahead, taps, mask]
    if out is not None:
        specs.append(pl.BlockSpec(memory_space=pl.ANY))
        args.append(out)
    return pl.pallas_call(
        functools.partial(rows_kernel, start, offset, width),
        in_specs=specs,
        out_specs=pl.BlockSpec(memory_space=pl.ANY),
        out_shape=jax.ShapeDtypeStruct((TOK, CH), BF),
        input_output_aliases={4: 0} if out is not None else {},
        scratch_shapes=[pltpu.VMEM((TOK, width), BF), pltpu.SemaphoreType.DMA(())],
        compiler_params=pltpu.CompilerParams(vmem_limit_bytes=ROOM),
        cost_estimate=pl.CostEstimate(flops=1 << 35, bytes_accessed=width << 10, transcendentals=0),
        name=f"rows_block_{start}",
    )(*args)


def sum_kernel(parts_ref, o_ref):
    total = parts_ref[0].astype(F32)
    for i in range(1, parts_ref.shape[0]):
        total = total + parts_ref[i].astype(F32)
    total = total.astype(BF)
    for i in range(o_ref.shape[0]):
        o_ref[i] = total


def summed(parts, copies):
    return pl.pallas_call(
        sum_kernel,
        in_specs=[VMEM],
        out_specs=VMEM,
        out_shape=jax.ShapeDtypeStruct((copies,) + parts.shape[1:], BF),
        compiler_params=pltpu.CompilerParams(vmem_limit_bytes=ROOM),
        cost_estimate=pl.CostEstimate(flops=1 << 35, bytes_accessed=parts.size * 2, transcendentals=0),
        name=f"sum_of_{parts.shape[0]}",
    )(parts)


def held_kernel(gate_ref, own_ref, gate_out, own_out, sems):
    copies = [
        pltpu.make_async_copy(gate_ref, gate_out, sems.at[0]),
        pltpu.make_async_copy(own_ref, own_out, sems.at[1]),
    ]
    for copy in copies:
        copy.start()
    for copy in copies:
        copy.wait()


def held(gate, own):
    block = jax.ShapeDtypeStruct((TOK, CH), BF)
    return pl.pallas_call(
        held_kernel,
        in_specs=[pl.BlockSpec(memory_space=pltpu.HBM)] * 2,
        out_specs=[VMEM] * 2,
        out_shape=[block, block],
        scratch_shapes=[pltpu.SemaphoreType.DMA((2,))],
        compiler_params=pltpu.CompilerParams(vmem_limit_bytes=4 * 1024 * 1024),
        cost_estimate=pl.CostEstimate(flops=1 << 30, bytes_accessed=4 << 20, transcendentals=0),
        name="held",
    )(gate, own)


def mask_kernel(base_ref, len_ref, ahead_ref, behind_ref):
    row = lax.broadcasted_iota(jnp.int32, (128, 128), 0)
    col = lax.broadcasted_iota(jnp.int32, (128, 128), 1)
    upto = (row <= col).astype(F32).astype(BF)
    lengths = jnp.broadcast_to(len_ref[...], (8, 128))
    high = lengths // 16
    low = lengths - 16 * high
    bounds = 16.0 * jnp.dot(high.astype(F32).astype(BF), upto, preferred_element_type=F32)
    bounds = bounds + jnp.dot(low.astype(F32).astype(BF), upto, preferred_element_type=F32)
    bounds = jnp.broadcast_to(bounds[0:1, :], (TOK, 128))
    base = base_ref[0, 0]
    here = (base + row).astype(F32)
    ended = bounds <= here
    end = jnp.min(jnp.where(ended, 2.0 * CH * TAPS, bounds), axis=1, keepdims=True)
    begin = jnp.max(jnp.where(ended, bounds, 0.0), axis=1, keepdims=True)
    source = base + jnp.where(col <= row, col, col - TOK)
    behind_ref[...] = (source.astype(F32) >= begin).astype(F32)
    own = (base + col).astype(F32)
    ahead_ref[:, :TOK] = jnp.where((col >= row) & (own < end), 1.0, 0.0).astype(BF)
    ahead_ref[:, TOK:] = jnp.where((col < row) & (own + 1.0 * TOK < end), 1.0, 0.0).astype(BF)


def masks(doc_lengths, base):
    return pl.pallas_call(
        mask_kernel,
        in_specs=[pl.BlockSpec(memory_space=pltpu.SMEM), VMEM],
        out_specs=[VMEM, VMEM],
        out_shape=[jax.ShapeDtypeStruct((TOK, 2 * TOK), BF), jax.ShapeDtypeStruct((TOK, TOK), F32)],
        compiler_params=pltpu.CompilerParams(vmem_limit_bytes=ROOM),
        name="masks",
    )(base.reshape(1, 1), doc_lengths.reshape(1, 128))


def last_sum_kernel(rows, parts_ref, o_ref):
    sets = FILT // rows
    for r in range(sets):
        total = parts_ref[r].astype(F32)
        for i in range(r + sets, parts_ref.shape[0], sets):
            total = total + parts_ref[i].astype(F32)
        o_ref[rows * r : rows * r + rows, :] = total


def last_sum(parts):
    return pl.pallas_call(
        functools.partial(last_sum_kernel, parts.shape[1]),
        in_specs=[VMEM],
        out_specs=VMEM,
        out_shape=jax.ShapeDtypeStruct((FILT, TAPS), F32),
        compiler_params=pltpu.CompilerParams(vmem_limit_bytes=ROOM),
        name="last_sum",
    )(parts)


def place(z, y, c):
    return (z * 8 + y) * 2 + c


PLANES = [[place(z + i, y, c) for i in range(2) for y in range(8) for c in range(2)] for z in range(0, 8, 2)]


def shifted(value, axis, steps, around=False):
    count = lax.axis_size(axis)
    pairs = [(i, i + steps) for i in range(count)]
    pairs = [(i, j % count) for i, j in pairs if around or 0 <= j < count]
    return lax.ppermute(value, axis, pairs)


def exchanged(value, groups):
    return lax.all_to_all(value, "ctx", 0, 0, axis_index_groups=groups)


def tied(value, *after):
    return lax.optimization_barrier((value, *after))[0]


def on_device(gate_values, conv_input, sent_grads, filter_taps, doc_lengths):
    gate, conv, sent, taps = gate_values[0], conv_input[0], sent_grads[0], filter_taps[0]
    base = lax.axis_index("ctx") * TOK
    half = CH // 2
    arrived = shifted(sent, "section", -1, around=True)
    behind = shifted(conv, "ctx", 1)
    gate, own = held(gate, conv)
    ahead_mask, behind_mask = masks(tied(doc_lengths, arrived), base)
    s0, s1, local = taps_sums(arrived, gate, behind, own, behind_mask, 32)
    got = exchanged(local, PLANES)
    ahead0 = shifted(s0, "ctx", -1)
    ahead1 = shifted(s1, "ctx", -1)
    got = exchanged(summed(got, 128), None)
    out = rows_block(s0, ahead0, taps, ahead_mask, None, 0, 0, half)
    out = rows_block(s1, ahead1, taps, ahead_mask, out, half, 0, half)
    filter_grad = last_sum(tied(got, out))[None]
    return out[None], filter_grad


def solution(mesh):
    return jax.shard_map(
        on_device,
        mesh=mesh,
        in_specs=(
            P("section", "ctx", None),
            P("section", "ctx", None),
            P("section", "ctx", None),
            P("section", None, None),
            P("section", None),
        ),
        out_specs=(P("section", "ctx", None), P("section", None, None)),
        check_vma=False,
    )
```
